32 devices in a mesh: ctx: 16 (over z, y, x), tp: 2 (over core).
Axes of the slice: x: 2, y: 2, z: 4, core: 2. Of those that a mesh axis runs over, the one named last changes fastest.
Arguments:
- inputs: bfloat16 [2048, 1024], P('ctx', 'tp'), may hold values from -6 to 6
- gate_in: bfloat16 [2048, 1024], P('ctx', 'tp'), may hold values from -6 to 6
- b_proj: bfloat16 [2048, 128], P('ctx'), may hold values from -0.5 to 0.5
- c_proj: bfloat16 [2048, 128], P('ctx'), may hold values from -0.5 to 0.5
- log_decay: float32 [8, 2048], P('tp', 'ctx'), may hold values from -0.75 to 0
- w_out: bfloat16 [1024, 4096], P('tp'), may hold values from -0.1875 to 0.1875
- cotangent: bfloat16 [2048, 4096], P(('ctx', 'tp')), may hold values from -6 to 6
Outputs:
- layer_out: bfloat16 [2048, 4096], P(('ctx', 'tp'))
- grad_inputs: bfloat16 [2048, 1024], P('ctx', 'tp')
- grad_gate: bfloat16 [2048, 1024], P('ctx', 'tp')
- grad_b: float32 [2048, 128], P(('ctx', 'tp'))
- grad_c: float32 [2048, 128], P(('ctx', 'tp'))
- grad_decay: float32 [8, 2048], P('tp', 'ctx')
The draws below stay inside these ranges and needn't reach their ends.
All inputs are finite; a program needn't handle non-finite values.
Results may differ from the reference program's by a relative error of at most 0.017.
Values may be sent and summed in bfloat16 or wider, within the bound.
A program may use at most 128 MiB of HBM per device.

```python
import jax
import jax.numpy as jnp
from jax import lax

D = 4096
P_SIZE = 128
NSTATE = 128
BLOCK = 128
TOK_DEV = 128
HEAD_TOTAL = 8
TOKEN_POSITIONS = 2048
N_TP = 2


def draw_log_decay(key, part):
    random_split_keys = jax.random.split(key, 7)
    ranking = jax.random.permutation(random_split_keys[0], HEAD_TOTAL)
    fast_count = HEAD_TOTAL // 2
    is_fast = ranking < fast_count
    fast_rate = jnp.exp(jax.random.uniform(random_split_keys[1], (HEAD_TOTAL,), jnp.float32, jnp.log(1.0 / 50.0), jnp.log(1.0 / 30.0)))
    slow_rate = jax.random.uniform(random_split_keys[2], (HEAD_TOTAL,), jnp.float32, 0.5, 1.0) * (0.5 / TOKEN_POSITIONS)
    baseline_rate = jnp.where(is_fast, fast_rate, slow_rate)
    block_count = TOKEN_POSITIONS // TOK_DEV
    block_multiplier = jnp.repeat(jax.random.uniform(random_split_keys[3], (HEAD_TOTAL, block_count), jnp.float32, 0.5, 1.0), TOK_DEV, axis=1)
    token_multiplier = jax.random.uniform(random_split_keys[4], (HEAD_TOTAL, TOKEN_POSITIONS), jnp.float32, 0.5, 1.5)
    spike_locations = jax.random.randint(random_split_keys[5], (2,), 0, TOKEN_POSITIONS)
    spike_flags = jnp.any(jnp.arange(TOKEN_POSITIONS)[None, :] == spike_locations[:, None], axis=0)
    spike_loss_value = jax.random.uniform(random_split_keys[6], (HEAD_TOTAL, TOKEN_POSITIONS), jnp.float32, 0.2, 0.5)
    return -baseline_rate[:, None] * block_multiplier * token_multiplier + jnp.where(spike_flags[None, :], jnp.log1p(-spike_loss_value), 0.0)


def shard_levels(own_key, shape, cuts, least, largest):
    def one(dim, parts):
        heights = jax.random.uniform(jax.random.fold_in(jax.random.fold_in(own_key, 6), dim), (parts,), jnp.float32, least / len(cuts), largest / len(cuts))
        return jnp.repeat(jnp.exp(heights), shape[dim] // parts).reshape((-1,) + (1,) * (len(shape) - dim - 1))

    loudness = one(*cuts[0])
    for cut in cuts[1:]:
        loudness = loudness * one(*cut)
    return loudness


def scatter_about(stream_key, dims, width, bound, shards=(), kind=jnp.bfloat16):
    gain = shard_levels(stream_key, dims, shards, -0.22, 0.18) if shards else 1.0
    values = jax.random.normal(stream_key, dims, jnp.float32) * width * gain
    return jnp.minimum(jnp.maximum(values, -bound), bound).astype(kind)


def setup_inputs(seed: int = 0) -> dict:
    arg_keys = jax.random.split(jax.random.key(seed), 8)
    return {
        "inputs": scatter_about(arg_keys[0], (TOKEN_POSITIONS, HEAD_TOTAL * P_SIZE), 1.0, 6.0, ((0, 16), (1, 2))),
        "gate_in": scatter_about(arg_keys[1], (TOKEN_POSITIONS, HEAD_TOTAL * P_SIZE), 1.0, 6.0, ((0, 16), (1, 2))),
        "b_proj": scatter_about(arg_keys[2], (TOKEN_POSITIONS, NSTATE), 0.08, 0.5, ((0, 16),)),
        "c_proj": scatter_about(arg_keys[3], (TOKEN_POSITIONS, NSTATE), 0.08, 0.5, ((0, 16),)),
        "log_decay": draw_log_decay(jax.random.fold_in(arg_keys[7], 71), 0),
        "w_out": scatter_about(arg_keys[5], (HEAD_TOTAL * P_SIZE, D), (HEAD_TOTAL * P_SIZE) ** -0.5, 0.1875, ((0, 2),)),
        "cotangent": scatter_about(arg_keys[6], (TOKEN_POSITIONS, D), 1.0, 6.0, ((0, 32),)),
    }


def block_pieces(x_block, b_block, c_block, d_block):
    length = d_block.shape[0]
    cumulative = jnp.cumsum(d_block, axis=0)
    final_sum = cumulative[-1]
    tail_weight = jnp.exp(final_sum[None, :] - cumulative)
    column_cum = cumulative.T
    differ = column_cum[:, :, None] - column_cum[:, None, :]
    position = jnp.arange(length)
    causal = position[:, None] >= position[None, :]
    decay_mat = jnp.where(causal[None], jnp.exp(jnp.minimum(differ, 0.0)), 0.0)
    scores = jnp.dot(c_block, b_block.T, preferred_element_type=jnp.float32)
    mixing_b = (scores[None] * decay_mat).astype(jnp.bfloat16)
    y_intra = jnp.einsum('hqk,khp->qhp', mixing_b.astype(jnp.float32), x_block.astype(jnp.float32))
    weighted = (x_block.astype(jnp.float32) * tail_weight[:, :, None]).astype(jnp.bfloat16)
    block_state = jnp.einsum('qhp,qn->hpn', weighted.astype(jnp.float32), b_block.astype(jnp.float32))
    return cumulative, tail_weight, decay_mat, scores, mixing_b, y_intra, weighted, block_state, jnp.exp(final_sum)


def reference(inputs, gate_in, b_proj, c_proj, log_decay, w_out, cotangent):
    total_len, feature_width = inputs.shape
    head_count = log_decay.shape[0]
    head_dim = feature_width // head_count
    nblocks = total_len // BLOCK
    x_blocks = inputs.reshape(nblocks, BLOCK, head_count, head_dim)
    z_blocks = gate_in.reshape(nblocks, BLOCK, head_count, head_dim)
    b_blocks = b_proj.reshape(nblocks, BLOCK, -1)
    c_blocks = c_proj.reshape(nblocks, BLOCK, -1)
    d_blocks = log_decay.reshape(head_count, nblocks, BLOCK).transpose(1, 2, 0)

    def first_pass(packed):
        pieces = block_pieces(*packed)
        return pieces[7], pieces[8]

    block_state, block_decay = lax.map(first_pass, (x_blocks, b_blocks, c_blocks, d_blocks))
    zero_state = jnp.zeros(block_state.shape[1:], jnp.float32)

    def chain_step(running, packed):
        decay_step, term_block = packed
        return decay_step[:, None, None] * running + term_block, running

    unused, state_in = lax.scan(chain_step, zero_state, (block_decay, block_state))

    def second_pass(packed):
        x_block, b_block, c_block, d_block, z_block, s_block = packed
        pieces = block_pieces(x_block, b_block, c_block, d_block)
        state_b = s_block.astype(jnp.bfloat16)
        y_inter = jnp.einsum('qn,hpn->qhp', c_block.astype(jnp.float32), state_b.astype(jnp.float32)) * jnp.exp(pieces[0])[:, :, None]
        y_full = pieces[5] + y_inter
        gated_out = (y_full * jax.nn.silu(z_block.astype(jnp.float32))).astype(jnp.bfloat16)
        return gated_out.reshape(BLOCK, feature_width)

    gated_out = lax.map(second_pass, (x_blocks, b_blocks, c_blocks, d_blocks, z_blocks, state_in)).reshape(total_len, feature_width)
    group_cols = feature_width // N_TP

    def add_group(running_sum, group_index):
        columns = lax.dynamic_slice_in_dim(gated_out, group_index * group_cols, group_cols, 1)
        weight_rows = lax.dynamic_slice_in_dim(w_out, group_index * group_cols, group_cols, 0)
        partial_sum = jnp.dot(columns, weight_rows, preferred_element_type=jnp.float32).astype(jnp.bfloat16)
        partial_sum = lax.optimization_barrier(partial_sum)
        return running_sum + partial_sum.astype(jnp.float32), None

    summed, unused = lax.scan(add_group, jnp.zeros((total_len, w_out.shape[1]), jnp.float32), jnp.arange(N_TP, dtype=jnp.int32))
    layer_out = summed.astype(jnp.bfloat16)
    dgated = jnp.dot(cotangent, w_out.T, preferred_element_type=jnp.float32).reshape(nblocks, BLOCK, head_count, head_dim)

    def adjoint_source(packed):
        c_block, d_block, z_block, g_block = packed
        cumulative = jnp.cumsum(d_block, axis=0)
        grad_y = g_block * jax.nn.silu(z_block.astype(jnp.float32))
        grad_w = (grad_y * jnp.exp(cumulative)[:, :, None]).astype(jnp.bfloat16)
        return jnp.einsum('qhp,qn->hpn', grad_w.astype(jnp.float32), c_block.astype(jnp.float32))

    injected = lax.map(adjoint_source, (c_blocks, d_blocks, z_blocks, dgated))
    unused, adjoint_next = lax.scan(chain_step, zero_state, (block_decay, injected), reverse=True)

    def third_pass(packed):
        x_block, b_block, c_block, d_block, z_block, g_block, s_block, r_block = packed
        cumulative, tail_weight, decay_mat, scores, mixing_b, y_intra, weighted, unused_state, block_dec = block_pieces(x_block, b_block, c_block, d_block)
        state_b = s_block.astype(jnp.bfloat16)
        adjoint_b = r_block.astype(jnp.bfloat16)
        y_inter = jnp.einsum('qn,hpn->qhp', c_block.astype(jnp.float32), state_b.astype(jnp.float32)) * jnp.exp(cumulative)[:, :, None]
        y_full = y_intra + y_inter
        gate_float = z_block.astype(jnp.float32)
        sigmoid_z = jax.nn.sigmoid(gate_float)
        grad_gate = (g_block * y_full * (sigmoid_z + gate_float * sigmoid_z * (1.0 - sigmoid_z))).astype(jnp.bfloat16)
        grad_y = g_block * gate_float * sigmoid_z
        grad_y_b = grad_y.astype(jnp.bfloat16)
        grad_w = (grad_y * jnp.exp(cumulative)[:, :, None]).astype(jnp.bfloat16)
        pair_dots = jnp.einsum('qhp,khp->hqk', grad_y_b.astype(jnp.float32), x_block.astype(jnp.float32))
        dmix = pair_dots * decay_mat
        dmix_b = dmix.astype(jnp.bfloat16).astype(jnp.float32)
        state_dx = jnp.einsum('kn,hpn->khp', b_block.astype(jnp.float32), adjoint_b.astype(jnp.float32)) * tail_weight[:, :, None]
        grad_inputs = (jnp.einsum('hqk,qhp->khp', mixing_b.astype(jnp.float32), grad_y_b.astype(jnp.float32)) + state_dx).astype(jnp.bfloat16)
        grad_b = jnp.einsum('hqk,qn->kn', dmix_b, c_block.astype(jnp.float32)) + jnp.einsum('khp,hpn->kn', weighted.astype(jnp.float32), adjoint_b.astype(jnp.float32))
        grad_c = jnp.einsum('hqk,kn->qn', dmix_b, b_block.astype(jnp.float32)) + jnp.einsum('qhp,hpn->qn', grad_w.astype(jnp.float32), state_b.astype(jnp.float32))
        cross_terms = dmix * scores[None]
        decay_flow = (jnp.sum(cross_terms, 2) - jnp.sum(cross_terms, 1)).T
        outflow = jnp.sum(x_block.astype(jnp.float32) * state_dx, 2)
        decay_flow = decay_flow + jnp.sum(grad_y * y_inter, 2) - outflow
        closing = jnp.sum(outflow, 0) + block_dec * jnp.sum(r_block * s_block, (1, 2))
        decay_flow = decay_flow.at[-1].add(closing)
        grad_decay = jnp.flip(jnp.cumsum(jnp.flip(decay_flow, 0), 0), 0)
        return grad_inputs.reshape(BLOCK, feature_width), grad_gate.reshape(BLOCK, feature_width), grad_b, grad_c, grad_decay.T

    results = lax.map(third_pass, (x_blocks, b_blocks, c_blocks, d_blocks, z_blocks, dgated, state_in, adjoint_next))
    grad_inputs = results[0].reshape(total_len, feature_width)
    grad_gate = results[1].reshape(total_len, feature_width)
    grad_b = results[2].reshape(total_len, -1)
    grad_c = results[3].reshape(total_len, -1)
    grad_decay = results[4].transpose(1, 0, 2).reshape(head_count, total_len)
    return layer_out, grad_inputs, grad_gate, grad_b, grad_c, grad_decay
```

```python
import functools

import jax
import jax.numpy as jnp
from jax import lax
from jax.experimental import pallas as pl
from jax.experimental.pallas import tpu as pltpu
from jax.sharding import PartitionSpec as P

BLOCK = 128
MESH = pl.DeviceIdType.MESH
F32, BF16 = jnp.float32, jnp.bfloat16
EXTRA = 16


def mm(a, b):
    return jnp.dot(a, b, preferred_element_type=F32)


def mm_nt(a, b, precision=None):
    return lax.dot_general(
        a, b, (((1,), (1,)), ((), ())), preferred_element_type=F32, precision=precision
    )


def mm_tn(a, b):
    return lax.dot_general(a, b, (((0,), (0,)), ((), ())), preferred_element_type=F32)


def two_parts(a):
    high = a.astype(BF16).astype(F32)
    shape = (EXTRA // 2, a.shape[1])
    rows = [jnp.broadcast_to(high, shape), jnp.broadcast_to(a - high, shape)]
    return jnp.concatenate(rows, axis=0).astype(BF16)


def kernel(
    sizes,
    x_hbm, g_hbm, b_hbm, c_hbm, ld_ref, w_hbm, cot_hbm,
    lo_out, gx_out, gg_out, gb_out, gc_out, gd_out,
    x_v, g_v, b_v, c_v, w_v, cot_v,
    cb_v, tail_v, expc_v, mask_v, wt_v, mix_v, sil_v, dsil_v, dg_v, gy_v, gyb_v, gw_v, y_v,
    gated_v, dmix_v, cross_v, yint_v, flow_v,
    msg1, rec1, loc, msg2, rec2, ent, msg3, st,
    lo_part, lo_rec, bc_part, bc_rec,
    lsem, cs, cr, s1s, s1r, s2s, s2r, s3s, s3r, ls, lr, bs, br,
):
    inner, outer, n_tp, w_chunks, lo_chunks = sizes
    heads = ld_ref.shape[0]
    width = x_v.shape[1]
    dim = width // heads
    nstate = b_v.shape[1]
    depth = w_v.shape[1]
    rows = cot_hbm.shape[0]
    part = width // inner
    place, tp = lax.axis_index("ctx"), lax.axis_index("tp")
    ip, zq = lax.rem(place, inner), lax.div(place, inner)
    mine = pl.multiple_of(tp * rows, rows)

    def lanes(h):
        return slice(h * dim, (h + 1) * dim)

    loads = [(x_hbm, x_v), (b_hbm, b_v), (c_hbm, c_v), (g_hbm, g_v)]
    loads.append((cot_hbm, cot_v.at[pl.ds(mine, rows)]))
    wrows = width // w_chunks
    for k in range(w_chunks):
        cut = pl.ds(k * wrows, wrows)
        loads.append((w_hbm.at[cut], w_v.at[cut]))
    loads = [pltpu.make_async_copy(s, d, lsem.at[i]) for i, (s, d) in enumerate(loads)]
    for copy in loads:
        copy.start()

    def plane(d):
        to = lax.rem(ip + d, inner)
        return to, (zq * inner + to, tp)

    def other(d):
        to = lax.rem(tp + d, n_tp)
        return to, (place, to)

    barrier = pltpu.get_barrier_semaphore()
    for d in range(1, n_tp):
        pl.semaphore_signal(barrier, inc=1, device_id=other(d)[1], device_id_type=MESH)
    for d in range(1, inner):
        pl.semaphore_signal(barrier, inc=1, device_id=plane(d)[1], device_id_type=MESH)
    for d in range(1, outer):
        to = lax.rem(zq + d, outer) * inner + ip
        pl.semaphore_signal(barrier, inc=1, device_id=(to, tp), device_id_type=MESH)
    pl.semaphore_wait(barrier, n_tp + inner + outer - 3)

    def remote(src, dst, ssem, rsem, device):
        return pltpu.make_async_remote_copy(
            src_ref=src, dst_ref=dst, send_sem=ssem, recv_sem=rsem,
            device_id=device, device_id_type=MESH,
        )

    cot_copies = [
        remote(cot_hbm, cot_v.at[pl.ds(mine, rows)], cs.at[d], cr.at[d], other(d)[1])
        for d in range(1, n_tp)
    ]
    for copy in cot_copies:
        copy.start()

    sends1, sends3 = {0: [], 1: []}, {0: [], 1: []}

    def start_plane(k, total, decays):
        for i in range(inner):
            msg1[k, i, 0:part, :] = total[i * part:(i + 1) * part].astype(BF16)
            msg1[k, i, part:part + EXTRA, :] = two_parts(decays[i * part // dim])
        for d in range(1, inner):
            to, device = plane(d)
            copy = remote(msg1.at[k, to], rec1.at[k, ip], s1s.at[k, d], s1r.at[k, d], device)
            copy.start()
            sends1[k].append(copy)
        rec1[k, pl.ds(ip, 1)] = msg1[k, pl.ds(ip, 1)]

    def z_copy(k, d):
        to = zq + d if k == 0 else zq - d
        return remote(
            msg2.at[k], rec2.at[k, zq], s2s.at[k, d], s2r.at[k, d], (to * inner + ip, tp)
        )

    def ahead(k, d):
        return zq + d < outer if k == 0 else zq - d >= 0

    def behind(k, d):
        return zq - d >= 0 if k == 0 else zq + d < outer

    def plane_scan(k):
        for copy in sends1[k]:
            copy.wait_recv()
        before = {}
        state = jnp.zeros((part, nstate), F32)
        decay = jnp.ones((1, nstate), F32)
        for p in range(inner) if k == 0 else reversed(range(inner)):
            loc[k, p] = state
            before[p] = decay
            own = rec1[k, p].astype(F32)
            step = own[part:part + 1] + own[part + EXTRA // 2:part + EXTRA // 2 + 1]
            state = step * state + own[0:part]
            decay = decay * step
        msg2[k, 0:part, :] = state.astype(BF16)
        msg2[k, part:part + EXTRA, :] = two_parts(decay)
        for d in range(1, outer):
            @pl.when(ahead(k, d))
            def _():
                z_copy(k, d).start()
        return before

    def z_scan(k, before):
        ent[k] = jnp.zeros((part, nstate), F32)
        for d in reversed(range(1, outer)):
            @pl.when(behind(k, d))
            def _():
                z_copy(k, d).wait_recv()
                own = rec2[k, zq - d if k == 0 else zq + d].astype(F32)
                step = own[part:part + 1] + own[part + EXTRA // 2:part + EXTRA // 2 + 1]
                ent[k] = step * ent[k] + own[0:part]
        entering = ent[k]
        for p in range(inner):
            msg3[k, p] = (before[p] * entering + loc[k, p]).astype(BF16)
        slot = pl.ds(pl.multiple_of(ip * part, part), part)
        for d in range(1, inner):
            to, device = plane(d)
            copy = remote(msg3.at[k, to], st.at[k, slot], s3s.at[k, d], s3r.at[k, d], device)
            copy.start()
            sends3[k].append(copy)
        st[k, slot, :] = msg3[k, pl.ds(ip, 1)].reshape(part, nstate)

    t_at = lax.broadcasted_iota(jnp.int32, (BLOCK, BLOCK), 0)
    s_at = lax.broadcasted_iota(jnp.int32, (BLOCK, BLOCK), 1)
    causal = t_at >= s_at
    lower = causal.astype(F32)
    steps = ld_ref[...]
    if heads % 8:
        steps = jnp.concatenate([steps, jnp.zeros((8 - heads % 8, BLOCK), F32)], axis=0)
    cum = mm_nt(steps, lower, lax.Precision.HIGHEST)
    decays = []
    loads[0].wait()
    loads[1].wait()
    for h in range(heads):
        column = jnp.transpose(jnp.broadcast_to(cum[h:h + 1], (BLOCK, BLOCK)))
        end = cum[h:h + 1, BLOCK - 1:BLOCK]
        tail = jnp.exp(end - column)
        cb_v[h] = column
        tail_v[h] = tail
        decays.append(jnp.broadcast_to(jnp.exp(end), (1, nstate)))
        wt_v[:, lanes(h)] = (x_v[:, lanes(h)].astype(F32) * tail).astype(BF16)
    start_plane(0, mm_tn(wt_v[...], b_v[...]), decays)

    loads[2].wait()
    loads[3].wait()
    for h in range(heads):
        expc_v[h] = jnp.exp(cb_v[h])
        v = g_v[:, lanes(h)].astype(F32)
        sig = 1.0 / (1.0 + jnp.exp(-v))
        sil_v[:, lanes(h)] = v * sig
        dsil_v[:, lanes(h)] = sig + v * sig * (1.0 - sig)
    scores = mm_nt(c_v[...], b_v[...])

    loads[4].wait()
    for copy in cot_copies:
        copy.wait_recv()
    before_f = None
    for k in range(w_chunks):
        loads[5 + k].wait()
        cut = slice(k * wrows, (k + 1) * wrows)
        dg_v[:, cut] = mm_nt(cot_v[...], w_v[cut, :])
        if k == 0:
            before_f = plane_scan(0)
    for h in range(heads):
        gy = dg_v[:, lanes(h)] * sil_v[:, lanes(h)]
        gy_v[:, lanes(h)] = gy
        gyb_v[:, lanes(h)] = gy.astype(BF16)
        gw_v[:, lanes(h)] = (gy * expc_v[h]).astype(BF16)
    start_plane(1, mm_tn(gw_v[...], c_v[...]), decays)

    for h in range(heads):
        column = cb_v[h]
        differ = column - jnp.broadcast_to(cum[h:h + 1], (BLOCK, BLOCK))
        mask = jnp.where(causal, jnp.exp(jnp.minimum(differ, 0.0)), 0.0)
        mask_v[h] = mask
        mix = (scores * mask).astype(BF16)
        mix_v[h] = mix
        y_v[:, lanes(h)] = mm(mix, x_v[:, lanes(h)])
    z_scan(0, before_f)
    before_b = plane_scan(1)

    total = jnp.zeros((BLOCK, BLOCK), F32)
    for h in range(heads):
        dmix = mm_nt(gyb_v[:, lanes(h)], x_v[:, lanes(h)]) * mask_v[h]
        total = total + dmix
        cross_v[h] = dmix * scores
    dmix_v[...] = total.astype(BF16)
    z_scan(1, before_b)

    for copy in sends3[0]:
        copy.wait_recv()
    y_inter = mm_nt(c_v[...], st[0])
    for h in range(heads):
        inter = y_inter[:, lanes(h)] * expc_v[h]
        yint_v[:, lanes(h)] = inter
        y = y_v[:, lanes(h)] + inter
        gated_v[:, lanes(h)] = (y * sil_v[:, lanes(h)]).astype(BF16)
        gg_out[:, lanes(h)] = (dg_v[:, lanes(h)] * y * dsil_v[:, lanes(h)]).astype(BF16)
    lcols = depth // lo_chunks
    lo_copies = []
    for k in range(lo_chunks):
        cut = slice(k * lcols, (k + 1) * lcols)
        lo_part[:, cut] = mm(gated_v[...], w_v[:, cut]).astype(BF16)
        for d in range(1, n_tp):
            to, device = other(d)
            theirs = pl.ds(pl.multiple_of(to * rows, rows), rows)
            copy = remote(
                lo_part.at[theirs, pl.ds(k * lcols, lcols)],
                lo_rec.at[d - 1, :, pl.ds(k * lcols, lcols)],
                ls.at[k, d], lr.at[k, d], device,
            )
            copy.start()
            lo_copies.append((k, d, copy))

    for copy in sends3[1]:
        copy.wait_recv()
    adj = st[1]
    bc_part[:, 0:nstate] = (mm_tn(dmix_v[...], c_v[...]) + mm(wt_v[...], adj)).astype(BF16)
    bc_part[:, nstate:2 * nstate] = (
        mm(dmix_v[...], b_v[...]) + mm(gw_v[...], st[0])
    ).astype(BF16)
    bc_copies = []
    for d in range(1, n_tp):
        to, device = other(d)
        theirs = pl.ds(pl.multiple_of(to * rows, rows), rows)
        copy = remote(bc_part.at[theirs], bc_rec.at[d - 1], bs.at[d], br.at[d], device)
        copy.start()
        bc_copies.append(copy)
    dx = mm_nt(b_v[...], adj)
    flow_v[...] = jnp.zeros(flow_v.shape, F32)
    last = lax.broadcasted_iota(jnp.int32, (1, BLOCK), 1) == BLOCK - 1
    for h in range(heads):
        state_dx = dx[:, lanes(h)] * tail_v[h]
        grad = mm_tn(mix_v[h], gyb_v[:, lanes(h)]) + state_dx
        gx_out[:, lanes(h)] = grad.astype(BF16)
        outflow = x_v[:, lanes(h)].astype(F32) * state_dx
        cross = cross_v[h]
        by_row = cross + gy_v[:, lanes(h)] * yint_v[:, lanes(h)] - outflow
        flow = jnp.sum(jnp.transpose(by_row) - cross, axis=0, keepdims=True)
        held = st[0, lanes(h), :].astype(F32) * st[1, lanes(h), :].astype(F32)
        closing = jnp.sum(outflow + decays[h] * held, axis=0, keepdims=True)
        closing = jnp.sum(closing, axis=1, keepdims=True)
        flow_v[h:h + 1, :] = flow + jnp.where(last, closing, 0.0)
    grad_decay = lax.dot_general(
        flow_v[...], lower, (((1,), (0,)), ((), ())),
        preferred_element_type=F32, precision=lax.Precision.HIGHEST,
    )
    gd_out[...] = grad_decay[0:heads]

    for k in range(lo_chunks):
        cut = slice(k * lcols, (k + 1) * lcols)
        out = lo_part[pl.ds(mine, rows), cut].astype(F32)
        for at, d, copy in lo_copies:
            if at == k:
                copy.wait_recv()
                out = out + lo_rec[d - 1, :, cut].astype(F32)
        lo_out[:, cut] = out.astype(BF16)
    both = bc_part[pl.ds(mine, rows), :].astype(F32)
    for d, copy in enumerate(bc_copies):
        copy.wait_recv()
        both = both + bc_rec[d].astype(F32)
    gb_out[...] = both[:, 0:nstate]
    gc_out[...] = both[:, nstate:2 * nstate]

    for copy in cot_copies + sends1[0] + sends1[1] + sends3[0] + sends3[1] + bc_copies:
        copy.wait_send()
    for _, _, copy in lo_copies:
        copy.wait_send()
    for k in range(2):
        for d in range(1, outer):
            @pl.when(ahead(k, d))
            def _():
                z_copy(k, d).wait_send()


def local(n_ctx, n_tp, inputs, gate_in, b_proj, c_proj, log_decay, w_out, cotangent):
    tok, width = inputs.shape
    heads = log_decay.shape[0]
    dim = width // heads
    nstate = b_proj.shape[1]
    rows, depth = cotangent.shape
    inner = 1
    while (2 * inner) ** 2 <= n_ctx and n_ctx % (2 * inner) == 0:
        inner *= 2
    inner = max(inner, min(heads, n_ctx))
    outer = n_ctx // inner
    part = width // inner
    assert tok == BLOCK and dim == BLOCK and nstate == BLOCK and dim % part == 0
    w_chunks, lo_chunks = 2, 4
    square = (heads, BLOCK, BLOCK)
    wide = (BLOCK, width)
    dma = pltpu.SemaphoreType.DMA
    scratch = [
        pltpu.VMEM(wide, BF16),
        pltpu.VMEM(wide, BF16),
        pltpu.VMEM((BLOCK, nstate), BF16),
        pltpu.VMEM((BLOCK, nstate), BF16),
        pltpu.VMEM((width, depth), BF16),
        pltpu.VMEM((BLOCK, depth), BF16),
        pltpu.VMEM(square, F32),
        pltpu.VMEM(square, F32),
        pltpu.VMEM(square, F32),
        pltpu.VMEM(square, F32),
        pltpu.VMEM(wide, BF16),
        pltpu.VMEM(square, BF16),
        pltpu.VMEM(wide, F32),
        pltpu.VMEM(wide, F32),
        pltpu.VMEM(wide, F32),
        pltpu.VMEM(wide, F32),
        pltpu.VMEM(wide, BF16),
        pltpu.VMEM(wide, BF16),
        pltpu.VMEM(wide, F32),
        pltpu.VMEM(wide, BF16),
        pltpu.VMEM((BLOCK, BLOCK), BF16),
        pltpu.VMEM(square, F32),
        pltpu.VMEM(wide, F32),
        pltpu.VMEM((-(-heads // 8) * 8, BLOCK), F32),
        pltpu.VMEM((2, inner, part + EXTRA, nstate), BF16),
        pltpu.VMEM((2, inner, part + EXTRA, nstate), BF16),
        pltpu.VMEM((2, inner, part, nstate), F32),
        pltpu.VMEM((2, part + EXTRA, nstate), BF16),
        pltpu.VMEM((2, outer, part + EXTRA, nstate), BF16),
        pltpu.VMEM((2, part, nstate), F32),
        pltpu.VMEM((2, inner, part, nstate), BF16),
        pltpu.VMEM((2, width, nstate), BF16),
        pltpu.VMEM((BLOCK, depth), BF16),
        pltpu.VMEM((max(n_tp - 1, 1), rows, depth), BF16),
        pltpu.VMEM((BLOCK, 2 * nstate), BF16),
        pltpu.VMEM((max(n_tp - 1, 1), rows, 2 * nstate), BF16),
        dma((5 + w_chunks,)),
        dma((n_tp,)), dma((n_tp,)),
        dma((2, inner)), dma((2, inner)),
        dma((2, outer)), dma((2, outer)),
        dma((2, inner)), dma((2, inner)),
        dma((lo_chunks, n_tp)), dma((lo_chunks, n_tp)),
        dma((n_tp,)), dma((n_tp,)),
    ]
    anywhere = pl.BlockSpec(memory_space=pl.ANY)
    vmem = pl.BlockSpec(memory_space=pltpu.VMEM)
    shape = jax.ShapeDtypeStruct
    return pl.pallas_call(
        functools.partial(kernel, (inner, outer, n_tp, w_chunks, lo_chunks)),
        out_shape=(
            shape((rows, depth), BF16),
            shape(wide, BF16),
            shape(wide, BF16),
            shape((rows, nstate), F32),
            shape((rows, nstate), F32),
            shape((heads, BLOCK), F32),
        ),
        in_specs=[anywhere] * 4 + [vmem] + [anywhere] * 2,
        out_specs=(vmem,) * 6,
        scratch_shapes=scratch,
        compiler_params=pltpu.CompilerParams(
            collective_id=0, has_side_effects=True, vmem_limit_bytes=40 * 1024 * 1024
        ),
        cost_estimate=pl.CostEstimate(
            flops=4 * BLOCK * width * depth, bytes_accessed=8 * 1024 * 1024, transcendentals=0
        ),
    )(inputs, gate_in, b_proj, c_proj, log_decay, w_out, cotangent)


def solution(mesh):
    in_specs = (
        P("ctx", "tp"),
        P("ctx", "tp"),
        P("ctx", None),
        P("ctx", None),
        P("tp", "ctx"),
        P("tp", None),
        P(("ctx", "tp"), None),
    )
    out_specs = (
        P(("ctx", "tp"), None),
        P("ctx", "tp"),
        P("ctx", "tp"),
        P(("ctx", "tp"), None),
        P(("ctx", "tp"), None),
        P("tp", "ctx"),
    )
    body = functools.partial(local, mesh.shape["ctx"], mesh.shape["tp"])
    return jax.shard_map(body, mesh=mesh, in_specs=in_specs, out_specs=out_specs, check_vma=False)
```

```python
import functools

import jax
import jax.numpy as jnp
from jax import lax
from jax.experimental import pallas as pl
from jax.experimental.pallas import tpu as pltpu
from jax.sharding import PartitionSpec as P

BLOCK = 128
MESH = pl.DeviceIdType.MESH
F32, BF16 = jnp.float32, jnp.bfloat16
EXTRA = 16


def mm(a, b):
    return jnp.dot(a, b, preferred_element_type=F32)


def mm_nt(a, b, precision=None):
    return lax.dot_general(
        a, b, (((1,), (1,)), ((), ())), preferred_element_type=F32, precision=precision
    )


def mm_tn(a, b):
    return lax.dot_general(a, b, (((0,), (0,)), ((), ())), preferred_element_type=F32)


def two_parts(a):
    high = a.astype(BF16).astype(F32)
    shape = (EXTRA // 2, a.shape[1])
    rows = [jnp.broadcast_to(high, shape), jnp.broadcast_to(a - high, shape)]
    return jnp.concatenate(rows, axis=0).astype(BF16)


def kernel(
    sizes,
    x_hbm, g_hbm, b_hbm, c_hbm, ld_ref, w_hbm, cot_hbm,
    lo_out, gx_out, gg_out, gb_out, gc_out, gd_out,
    x_v, g_v, b_v, c_v, w_v, cot_v,
    cb_v, tail_v, expc_v, mask_v, wt_v, mix_v, sil_v, dsil_v, dg_v, gy_v, gyb_v, gw_v, y_v,
    gated_v, dmix_v, cross_v, yint_v, flow_v,
    msg1, rec1, loc, msg2, rec2, ent, msg3, st,
    lo_part, lo_rec, bc_part, bc_rec,
    lsem, cs, cr, s1s, s1r, s2s, s2r, s3s, s3r, ls, lr, bs, br,
):
    inner, outer, n_tp, w_chunks, lo_chunks = sizes
    heads = ld_ref.shape[0]
    width = x_v.shape[1]
    dim = width // heads
    nstate = b_v.shape[1]
    depth = w_v.shape[1]
    rows = cot_hbm.shape[0]
    part = width // inner
    place, tp = lax.axis_index("ctx"), lax.axis_index("tp")
    ip, zq = lax.rem(place, inner), lax.div(place, inner)
    mine = pl.multiple_of(tp * rows, rows)

    def lanes(h):
        return slice(h * dim, (h + 1) * dim)

    loads = [(x_hbm, x_v), (b_hbm, b_v), (c_hbm, c_v), (g_hbm, g_v)]
    loads.append((cot_hbm, cot_v.at[pl.ds(mine, rows)]))
    wrows = width // w_chunks
    for k in range(w_chunks):
        cut = pl.ds(k * wrows, wrows)
        loads.append((w_hbm.at[cut], w_v.at[cut]))
    loads = [pltpu.make_async_copy(s, d, lsem.at[i]) for i, (s, d) in enumerate(loads)]
    for copy in loads:
        copy.start()

    def plane(d):
        to = lax.rem(ip + d, inner)
        return to, (zq * inner + to, tp)

    def other(d):
        to = lax.rem(tp + d, n_tp)
        return to, (place, to)

    barrier = pltpu.get_barrier_semaphore()
    for d in range(1, n_tp):
        pl.semaphore_signal(barrier, inc=1, device_id=other(d)[1], device_id_type=MESH)
    for d in range(1, inner):
        pl.semaphore_signal(barrier, inc=1, device_id=plane(d)[1], device_id_type=MESH)
    for d in range(1, outer):
        to = lax.rem(zq + d, outer) * inner + ip
        pl.semaphore_signal(barrier, inc=1, device_id=(to, tp), device_id_type=MESH)
    pl.semaphore_wait(barrier, n_tp + inner + outer - 3)

    def remote(src, dst, ssem, rsem, device):
        return pltpu.make_async_remote_copy(
            src_ref=src, dst_ref=dst, send_sem=ssem, recv_sem=rsem,
            device_id=device, device_id_type=MESH,
        )

    cot_copies = [
        remote(cot_hbm, cot_v.at[pl.ds(mine, rows)], cs.at[d], cr.at[d], other(d)[1])
        for d in range(1, n_tp)
    ]
    for copy in cot_copies:
        copy.start()

    sends1, sends3 = {0: [], 1: []}, {0: [], 1: []}

    def start_plane(k, total, decays):
        for i in range(inner):
            msg1[k, i, 0:part, :] = total[i * part:(i + 1) * part].astype(BF16)
            msg1[k, i, part:part + EXTRA, :] = two_parts(decays[i * part // dim])
        for d in range(1, inner):
            to, device = plane(d)
            copy = remote(msg1.at[k, to], rec1.at[k, ip], s1s.at[k, d], s1r.at[k, d], device)
            copy.start()
            sends1[k].append(copy)
        rec1[k, pl.ds(ip, 1)] = msg1[k, pl.ds(ip, 1)]

    def z_copy(k, d):
        to = zq + d if k == 0 else zq - d
        return remote(
            msg2.at[k], rec2.at[k, zq], s2s.at[k, d], s2r.at[k, d], (to * inner + ip, tp)
        )

    def ahead(k, d):
        return zq + d < outer if k == 0 else zq - d >= 0

    def behind(k, d):
        return zq - d >= 0 if k == 0 else zq + d < outer

    def plane_scan(k):
        for copy in sends1[k]:
            copy.wait_recv()
        before = {}
        state = jnp.zeros((part, nstate), F32)
        decay = jnp.ones((1, nstate), F32)
        for p in range(inner) if k == 0 else reversed(range(inner)):
            loc[k, p] = state
            before[p] = decay
            own = rec1[k, p].astype(F32)
            step = own[part:part + 1] + own[part + EXTRA // 2:part + EXTRA // 2 + 1]
            state = step * state + own[0:part]
            decay = decay * step
        msg2[k, 0:part, :] = state.astype(BF16)
        msg2[k, part:part + EXTRA, :] = two_parts(decay)
        for d in range(1, outer):
            @pl.when(ahead(k, d))
            def _():
                z_copy(k, d).start()
        return before

    def z_scan(k, before):
        ent[k] = jnp.zeros((part, nstate), F32)
        for d in reversed(range(1, outer)):
            @pl.when(behind(k, d))
            def _():
                z_copy(k, d).wait_recv()
                own = rec2[k, zq - d if k == 0 else zq + d].astype(F32)
                step = own[part:part + 1] + own[part + EXTRA // 2:part + EXTRA // 2 + 1]
                ent[k] = step * ent[k] + own[0:part]
        entering = ent[k]
        for p in range(inner):
            msg3[k, p] = (before[p] * entering + loc[k, p]).astype(BF16)
        slot = pl.ds(pl.multiple_of(ip * part, part), part)
        for d in range(1, inner):
            to, device = plane(d)
            copy = remote(msg3.at[k, to], st.at[k, slot], s3s.at[k, d], s3r.at[k, d], device)
            copy.start()
            sends3[k].append(copy)
        st[k, slot, :] = msg3[k, pl.ds(ip, 1)].reshape(part, nstate)

    t_at = lax.broadcasted_iota(jnp.int32, (BLOCK, BLOCK), 0)
    s_at = lax.broadcasted_iota(jnp.int32, (BLOCK, BLOCK), 1)
    causal = t_at >= s_at
    lower = causal.astype(F32)
    steps = ld_ref[...]
    if heads % 8:
        steps = jnp.concatenate([steps, jnp.zeros((8 - heads % 8, BLOCK), F32)], axis=0)
    cum = mm_nt(steps, lower, lax.Precision.HIGHEST)
    decays = []
    loads[0].wait()
    loads[1].wait()
    for h in range(heads):
        column = jnp.transpose(jnp.broadcast_to(cum[h:h + 1], (BLOCK, BLOCK)))
        end = cum[h:h + 1, BLOCK - 1:BLOCK]
        tail = jnp.exp(end - column)
        cb_v[h] = column
        tail_v[h] = tail
        decays.append(jnp.broadcast_to(jnp.exp(end), (1, nstate)))
        wt_v[:, lanes(h)] = (x_v[:, lanes(h)].astype(F32) * tail).astype(BF16)
    start_plane(0, mm_tn(wt_v[...], b_v[...]), decays)

    loads[2].wait()
    loads[3].wait()
    for h in range(heads):
        expc_v[h] = jnp.exp(cb_v[h])
        v = g_v[:, lanes(h)].astype(F32)
        sig = 1.0 / (1.0 + jnp.exp(-v))
        sil_v[:, lanes(h)] = v * sig
        dsil_v[:, lanes(h)] = sig + v * sig * (1.0 - sig)
    scores = mm_nt(c_v[...], b_v[...])

    loads[4].wait()
    for copy in cot_copies:
        copy.wait_recv()
    before_f = None
    for k in range(w_chunks):
        loads[5 + k].wait()
        cut = slice(k * wrows, (k + 1) * wrows)
        dg_v[:, cut] = mm_nt(cot_v[...], w_v[cut, :])
        if k == 0:
            before_f = plane_scan(0)
    for h in range(heads):
        gy = dg_v[:, lanes(h)] * sil_v[:, lanes(h)]
        gy_v[:, lanes(h)] = gy
        gyb_v[:, lanes(h)] = gy.astype(BF16)
        gw_v[:, lanes(h)] = (gy * expc_v[h]).astype(BF16)
    start_plane(1, mm_tn(gw_v[...], c_v[...]), decays)

    for h in range(heads):
        column = cb_v[h]
        differ = column - jnp.broadcast_to(cum[h:h + 1], (BLOCK, BLOCK))
        mask = jnp.where(causal, jnp.exp(jnp.minimum(differ, 0.0)), 0.0)
        mask_v[h] = mask
        mix = (scores * mask).astype(BF16)
        mix_v[h] = mix
        y_v[:, lanes(h)] = mm(mix, x_v[:, lanes(h)])
    z_scan(0, before_f)
    before_b = plane_scan(1)

    total = jnp.zeros((BLOCK, BLOCK), F32)
    for h in range(heads):
        dmix = mm_nt(gyb_v[:, lanes(h)], x_v[:, lanes(h)]) * mask_v[h]
        total = total + dmix
        cross_v[h] = dmix * scores
    dmix_v[...] = total.astype(BF16)
    z_scan(1, before_b)

    for copy in sends3[0]:
        copy.wait_recv()
    y_inter = mm_nt(c_v[...], st[0])
    for h in range(heads):
        inter = y_inter[:, lanes(h)] * expc_v[h]
        yint_v[:, lanes(h)] = inter
        y = y_v[:, lanes(h)] + inter
        gated_v[:, lanes(h)] = (y * sil_v[:, lanes(h)]).astype(BF16)
        gg_out[:, lanes(h)] = (dg_v[:, lanes(h)] * y * dsil_v[:, lanes(h)]).astype(BF16)
    lcols = depth // lo_chunks
    lo_copies = []
    for k in range(lo_chunks):
        cut = slice(k * lcols, (k + 1) * lcols)
        lo_part[:, cut] = mm(gated_v[...], w_v[:, cut]).astype(BF16)
        for d in range(1, n_tp):
            to, device = other(d)
            theirs = pl.ds(pl.multiple_of(to * rows, rows), rows)
            copy = remote(
                lo_part.at[theirs, pl.ds(k * lcols, lcols)],
                lo_rec.at[d - 1, :, pl.ds(k * lcols, lcols)],
                ls.at[k, d], lr.at[k, d], device,
            )
            copy.start()
            lo_copies.append((k, d, copy))

    for copy in sends3[1]:
        copy.wait_recv()
    adj = st[1]
    bc_part[:, 0:nstate] = (mm_tn(dmix_v[...], c_v[...]) + mm(wt_v[...], adj)).astype(BF16)
    bc_part[:, nstate:2 * nstate] = (
        mm(dmix_v[...], b_v[...]) + mm(gw_v[...], st[0])
    ).astype(BF16)
    bc_copies = []
    for d in range(1, n_tp):
        to, device = other(d)
        theirs = pl.ds(pl.multiple_of(to * rows, rows), rows)
        copy = remote(bc_part.at[theirs], bc_rec.at[d - 1], bs.at[d], br.at[d], device)
        copy.start()
        bc_copies.append(copy)
    dx = mm_nt(b_v[...], adj)
    flow_v[...] = jnp.zeros(flow_v.shape, F32)
    last = lax.broadcasted_iota(jnp.int32, (1, BLOCK), 1) == BLOCK - 1
    for h in range(heads):
        state_dx = dx[:, lanes(h)] * tail_v[h]
        grad = mm_tn(mix_v[h], gyb_v[:, lanes(h)]) + state_dx
        gx_out[:, lanes(h)] = grad.astype(BF16)
        outflow = x_v[:, lanes(h)].astype(F32) * state_dx
        cross = cross_v[h]
        by_row = cross + gy_v[:, lanes(h)] * yint_v[:, lanes(h)] - outflow
        flow = jnp.sum(jnp.transpose(by_row) - cross, axis=0, keepdims=True)
        held = st[0, lanes(h), :].astype(F32) * st[1, lanes(h), :].astype(F32)
        closing = jnp.sum(outflow + decays[h] * held, axis=0, keepdims=True)
        closing = jnp.sum(closing, axis=1, keepdims=True)
        flow_v[h:h + 1, :] = flow + jnp.where(last, closing, 0.0)
    grad_decay = lax.dot_general(
        flow_v[...], lower, (((1,), (0,)), ((), ())),
        preferred_element_type=F32, precision=lax.Precision.HIGHEST,
    )
    gd_out[...] = grad_decay[0:heads]

    for k in range(lo_chunks):
        cut = slice(k * lcols, (k + 1) * lcols)
        out = lo_part[pl.ds(mine, rows), cut].astype(F32)
        for at, d, copy in lo_copies:
            if at == k:
                copy.wait_recv()
                out = out + lo_rec[d - 1, :, cut].astype(F32)
        lo_out[:, cut] = out.astype(BF16)
    both = bc_part[pl.ds(mine, rows), :].astype(F32)
    for d, copy in enumerate(bc_copies):
        copy.wait_recv()
        both = both + bc_rec[d].astype(F32)
    gb_out[...] = both[:, 0:nstate]
    gc_out[...] = both[:, nstate:2 * nstate]

    for copy in cot_copies + sends1[0] + sends1[1] + sends3[0] + sends3[1] + bc_copies:
        copy.wait_send()
    for _, _, copy in lo_copies:
        copy.wait_send()
    for k in range(2):
        for d in range(1, outer):
            @pl.when(ahead(k, d))
            def _():
                z_copy(k, d).wait_send()


def hand_over(*refs):
    count = len(refs) // 2
    sems = refs[-1]
    copies = [
        pltpu.make_async_copy(refs[i], refs[count + i], sems.at[i]) for i in range(count)
    ]
    for copy in copies:
        copy.start()
    for copy in copies:
        copy.wait()


def local(n_ctx, n_tp, inputs, gate_in, b_proj, c_proj, log_decay, w_out, cotangent):
    tok, width = inputs.shape
    heads = log_decay.shape[0]
    dim = width // heads
    nstate = b_proj.shape[1]
    rows, depth = cotangent.shape
    inner = 1
    while (2 * inner) ** 2 <= n_ctx and n_ctx % (2 * inner) == 0:
        inner *= 2
    inner = max(inner, min(heads, n_ctx))
    outer = n_ctx // inner
    part = width // inner
    assert tok == BLOCK and dim == BLOCK and nstate == BLOCK and dim % part == 0
    w_chunks, lo_chunks = 2, 4
    square = (heads, BLOCK, BLOCK)
    wide = (BLOCK, width)
    dma = pltpu.SemaphoreType.DMA
    scratch = [
        pltpu.VMEM(wide, BF16),
        pltpu.VMEM(wide, BF16),
        pltpu.VMEM((BLOCK, nstate), BF16),
        pltpu.VMEM((BLOCK, nstate), BF16),
        pltpu.VMEM((width, depth), BF16),
        pltpu.VMEM((BLOCK, depth), BF16),
        pltpu.VMEM(square, F32),
        pltpu.VMEM(square, F32),
        pltpu.VMEM(square, F32),
        pltpu.VMEM(square, F32),
        pltpu.VMEM(wide, BF16),
        pltpu.VMEM(square, BF16),
        pltpu.VMEM(wide, F32),
        pltpu.VMEM(wide, F32),
        pltpu.VMEM(wide, F32),
        pltpu.VMEM(wide, F32),
        pltpu.VMEM(wide, BF16),
        pltpu.VMEM(wide, BF16),
        pltpu.VMEM(wide, F32),
        pltpu.VMEM(wide, BF16),
        pltpu.VMEM((BLOCK, BLOCK), BF16),
        pltpu.VMEM(square, F32),
        pltpu.VMEM(wide, F32),
        pltpu.VMEM((-(-heads // 8) * 8, BLOCK), F32),
        pltpu.VMEM((2, inner, part + EXTRA, nstate), BF16),
        pltpu.VMEM((2, inner, part + EXTRA, nstate), BF16),
        pltpu.VMEM((2, inner, part, nstate), F32),
        pltpu.VMEM((2, part + EXTRA, nstate), BF16),
        pltpu.VMEM((2, outer, part + EXTRA, nstate), BF16),
        pltpu.VMEM((2, part, nstate), F32),
        pltpu.VMEM((2, inner, part, nstate), BF16),
        pltpu.VMEM((2, width, nstate), BF16),
        pltpu.VMEM((BLOCK, depth), BF16),
        pltpu.VMEM((max(n_tp - 1, 1), rows, depth), BF16),
        pltpu.VMEM((BLOCK, 2 * nstate), BF16),
        pltpu.VMEM((max(n_tp - 1, 1), rows, 2 * nstate), BF16),
        dma((5 + w_chunks,)),
        dma((n_tp,)), dma((n_tp,)),
        dma((2, inner)), dma((2, inner)),
        dma((2, outer)), dma((2, outer)),
        dma((2, inner)), dma((2, inner)),
        dma((lo_chunks, n_tp)), dma((lo_chunks, n_tp)),
        dma((n_tp,)), dma((n_tp,)),
    ]
    anywhere = pl.BlockSpec(memory_space=pl.ANY)
    vmem = pl.BlockSpec(memory_space=pltpu.VMEM)
    shape = jax.ShapeDtypeStruct
    results = pl.pallas_call(
        functools.partial(kernel, (inner, outer, n_tp, w_chunks, lo_chunks)),
        out_shape=(
            shape((rows, depth), BF16),
            shape(wide, BF16),
            shape(wide, BF16),
            shape((rows, nstate), F32),
            shape((rows, nstate), F32),
            shape((heads, BLOCK), F32),
        ),
        in_specs=[anywhere] * 4 + [vmem] + [anywhere] * 2,
        out_specs=(vmem,) * 6,
        scratch_shapes=scratch,
        compiler_params=pltpu.CompilerParams(
            collective_id=0, has_side_effects=True, vmem_limit_bytes=56 * 1024 * 1024
        ),
        cost_estimate=pl.CostEstimate(
            flops=4 * BLOCK * width * depth, bytes_accessed=8 * 1024 * 1024, transcendentals=0
        ),
    )(inputs, gate_in, b_proj, c_proj, log_decay, w_out, cotangent)
    return pl.pallas_call(
        hand_over,
        out_shape=[shape(r.shape, r.dtype) for r in results],
        in_specs=[anywhere] * 6,
        out_specs=(anywhere,) * 6,
        scratch_shapes=[dma((6,))],
        compiler_params=pltpu.CompilerParams(vmem_limit_bytes=56 * 1024 * 1024),
        cost_estimate=pl.CostEstimate(flops=0, bytes_accessed=2 * 1024 * 1024, transcendentals=0),
    )(*results)


def solution(mesh):
    in_specs = (
        P("ctx", "tp"),
        P("ctx", "tp"),
        P("ctx", None),
        P("ctx", None),
        P("tp", "ctx"),
        P("tp", None),
        P(("ctx", "tp"), None),
    )
    out_specs = (
        P(("ctx", "tp"), None),
        P("ctx", "tp"),
        P("ctx", "tp"),
        P(("ctx", "tp"), None),
        P(("ctx", "tp"), None),
        P("tp", "ctx"),
    )
    body = functools.partial(local, mesh.shape["ctx"], mesh.shape["tp"])
    return jax.shard_map(body, mesh=mesh, in_specs=in_specs, out_specs=out_specs, check_vma=False)
```
